32 devices in a mesh: dp: 8 (over z, x), mp: 4 (over y, core).
Axes of the slice: x: 2, y: 2, z: 4, core: 2. Of those that a mesh axis runs over, the one named last changes fastest.
Arguments:
- queries: bfloat16 [2048, 4096], P('dp', 'mp'), may hold values from -6 to 6
- keys: bfloat16 [2048, 4096], P('dp', 'mp'), may hold values from -6 to 6
- values: bfloat16 [2048, 4096], P('dp', 'mp'), may hold values from -12 to 12
- cotangent: bfloat16 [2048, 6144], P(('dp', 'mp')), may hold values from -0.796875 to 0.796875
- master: float32 [4096, 6144], P('mp', 'dp'), may hold values from -0.09375 to 0.09375
- moment_one: float32 [4096, 6144], P('mp', 'dp'), may hold values from -6 to 6
- moment_two: float32 [4096, 6144], P('mp', 'dp'), may hold values from 1 to 10
Outputs:
- attn_out: bfloat16 [2048, 6144], P(('dp', 'mp'))
- grad_queries: bfloat16 [2048, 4096], P('dp', 'mp')
- grad_keys: bfloat16 [2048, 4096], P('dp', 'mp')
- grad_values: bfloat16 [2048, 4096], P('dp', 'mp')
- new_master: float32 [4096, 6144], P('mp', 'dp')
- new_moment_one: float32 [4096, 6144], P('mp', 'dp')
- new_moment_two: float32 [4096, 6144], P('mp', 'dp')
The draws below stay inside these ranges and needn't reach their ends.
All inputs are finite; a program needn't handle non-finite values.
Results may differ from the reference program's by a relative error of at most 0.014.
Values may be sent and summed in bfloat16 or wider, within the bound.
A program may use at most 128 MiB of HBM per device.

```python
import math
import jax
import jax.numpy as jnp
from jax import lax

D = 6144
HEADS = 32
HEAD_DIM = 128
PATCHES = 256
TOKENS = 2048
N_DP = 8


def draw_queries(key, part):
    key = jax.random.fold_in(key, 11)
    shape = (TOKENS, HEADS * HEAD_DIM)
    base = jnp.clip(jax.random.normal(key, shape, jnp.float32), -6.0, 6.0)
    return base.astype(jnp.bfloat16)


def draw_keys(key, part):
    key = jax.random.fold_in(key, 23)
    shape = (TOKENS, HEADS * HEAD_DIM)
    base = jnp.clip(jax.random.normal(key, shape, jnp.float32), -6.0, 6.0)
    return base.astype(jnp.bfloat16)


def with_spikes(values, rng, source, target, blocks, factor):
    def block_of(dim):
        return (jnp.arange(values.shape[dim]) // (values.shape[dim] // blocks)).reshape((-1,) + (1,) * (values.ndim - 1 - dim))

    near = jax.random.permutation(rng, blocks)[block_of(target)]
    other_side = (block_of(target) + blocks // 2) % blocks
    return jnp.where((block_of(source) == near) | (block_of(source) == other_side), factor * values, values)


def shard_levels(key, extent, cuts, least, largest):
    gain, own = 1.0, jax.random.fold_in(key, 6)
    for dim, shards_of in cuts:
        heights = jnp.exp(jax.random.uniform(jax.random.fold_in(own, dim), (shards_of,), jnp.float32, least / len(cuts), largest / len(cuts)))
        gain = gain * jnp.repeat(heights, extent[dim] // shards_of).reshape([-1 if axis == dim else 1 for axis in range(len(extent))])
    return gain


def centred(rng, dims, scale, reach, shards=(), held_as=jnp.bfloat16):
    values = scale * jax.random.normal(rng, dims, jnp.float32)
    if shards:
        values = values * shard_levels(rng, dims, shards, -0.22, 0.18)
    return jnp.clip(values, -reach, reach).astype(held_as)


def gaussian_with(own_key, shape, scale, bound, pieces, heavy, dtype=jnp.bfloat16):
    result = scale * jax.random.normal(own_key, shape, jnp.float32)
    if pieces:
        result = result * shard_levels(own_key, shape, pieces, -0.22, 0.18)
    return jnp.clip(with_spikes(result, jax.random.fold_in(own_key, 3), *heavy), -bound, bound).astype(dtype)


def setup_inputs(seed: int = 0) -> dict:
    splits = jax.random.split(jax.random.key(seed), 8)
    return {
        "queries": draw_queries(jax.random.fold_in(splits[7], 71), 0),
        "keys": draw_keys(jax.random.fold_in(splits[7], 71), 0),
        "values": centred(splits[2], (TOKENS, HEADS * HEAD_DIM), 3.0, 12.0, ((0, 8), (1, 4))),
        "cotangent": gaussian_with(splits[3], (TOKENS, D), 0.1, 0.796875, ((0, 32),), (0, 1, 32, 2.75)),
        "master": centred(splits[4], (HEADS * HEAD_DIM, D), (HEADS * HEAD_DIM) ** -0.5, 0.09375, ((0, 4), (1, 8)), jnp.float32),
        "moment_one": centred(splits[5], (HEADS * HEAD_DIM, D), 1.0, 6.0, ((0, 4), (1, 8)), jnp.float32),
        "moment_two": jnp.clip(jnp.exp(math.log(10.0) - 2.3025851 * jax.random.uniform(splits[6], (HEADS * HEAD_DIM, D), jnp.float32) ** shard_levels(splits[6], (HEADS * HEAD_DIM, D), ((0, 4), (1, 8)), -0.2, 0.2)), 1.0, 10.0),
    }


def image_forward(query_img, key_img, value_img):
    scaling = HEAD_DIM ** (-0.5)
    scores = jnp.einsum('phd,qhd->hpq', query_img.astype(jnp.float32), key_img.astype(jnp.float32)) * scaling
    probs = jax.nn.softmax(scores, axis=-1)
    probs_b = probs.astype(jnp.bfloat16)
    context = jnp.einsum('hpq,qhd->phd', probs_b.astype(jnp.float32), value_img.astype(jnp.float32))
    return context.astype(jnp.bfloat16)

def image_backward(query_img, key_img, value_img, dctx_img):
    scaling = HEAD_DIM ** (-0.5)
    scores = jnp.einsum('phd,qhd->hpq', query_img.astype(jnp.float32), key_img.astype(jnp.float32)) * scaling
    probs = jax.nn.softmax(scores, axis=-1)
    probs_b = probs.astype(jnp.bfloat16)
    grad_probs = jnp.einsum('phd,qhd->hpq', dctx_img.astype(jnp.float32), value_img.astype(jnp.float32))
    inner = lax.optimization_barrier(jnp.sum(probs * grad_probs, axis=-1, keepdims=True))
    grad_scores = (probs * (grad_probs - inner) * scaling).astype(jnp.bfloat16).astype(jnp.float32)
    grad_q = jnp.einsum('hpq,qhd->phd', grad_scores, key_img.astype(jnp.float32))
    grad_k = jnp.einsum('hpq,phd->qhd', grad_scores, query_img.astype(jnp.float32))
    grad_v = jnp.einsum('hpq,phd->qhd', probs_b.astype(jnp.float32), dctx_img.astype(jnp.float32))
    return (grad_q.astype(jnp.bfloat16), grad_k.astype(jnp.bfloat16), grad_v.astype(jnp.bfloat16))

def reference(queries, keys, values, cotangent, master, moment_one, moment_two):
    images = TOKENS // PATCHES
    shaped = (images, PATCHES, HEADS, HEAD_DIM)
    query_all = queries.reshape(shaped)
    key_all = keys.reshape(shaped)
    value_all = values.reshape(shaped)
    weight = master.astype(jnp.bfloat16)
    context = lax.map(lambda group: image_forward(group[0], group[1], group[2]), (query_all, key_all, value_all))
    context = context.reshape(TOKENS, HEADS * HEAD_DIM)
    attn_out = jnp.dot(context, weight, preferred_element_type=jnp.float32).astype(jnp.bfloat16)
    grad_context = jnp.dot(cotangent, weight.T, preferred_element_type=jnp.float32).astype(jnp.bfloat16)
    ctx_groups = context.reshape(N_DP, TOKENS // N_DP, HEADS * HEAD_DIM)
    cot_groups = cotangent.reshape(N_DP, TOKENS // N_DP, D)

    def add_group(total, pair):
        part = jnp.dot(pair[0].T, pair[1], preferred_element_type=jnp.float32).astype(jnp.bfloat16)
        part = lax.optimization_barrier(part)
        return (total + part.astype(jnp.float32), None)
    grad_weight, unused = lax.scan(add_group, jnp.zeros((HEADS * HEAD_DIM, D), jnp.float32), (ctx_groups, cot_groups))
    new_one = 0.9 * moment_one + 0.1 * grad_weight
    new_two = 0.95 * moment_two + 0.05 * grad_weight * grad_weight
    new_master = master - 0.001 * (new_one / 0.19) / (jnp.sqrt(new_two / 0.0975) + 1e-08)
    dctx_all = grad_context.reshape(shaped)
    grad_q, grad_k, grad_v = lax.map(lambda group: image_backward(group[0], group[1], group[2], group[3]), (query_all, key_all, value_all, dctx_all))
    flat = (TOKENS, HEADS * HEAD_DIM)
    return (attn_out, grad_q.reshape(flat), grad_k.reshape(flat), grad_v.reshape(flat), new_master, new_one, new_two)
```

```python
import functools

import jax
import jax.numpy as jnp
from jax import lax
from jax.experimental import pallas as pl
from jax.experimental.pallas import tpu as pltpu
from jax.sharding import PartitionSpec as P

HEAD_DIM = 128
PATCHES = 256
PAIR = 2
SCALING = HEAD_DIM ** (-0.5)
NT = (((1,), (1,)), ((), ()))
TN = (((0,), (0,)), ((), ()))


def dot(x, y, dims=(((1,), (0,)), ((), ()))):
    return lax.dot_general(x, y, dims, preferred_element_type=jnp.float32)


def softmax_of(q, k):
    scores = dot(q, k, NT) * SCALING
    e = jnp.exp(scores - jnp.max(scores, axis=-1, keepdims=True))
    return e / jnp.sum(e, axis=-1, keepdims=True)


def forward_kernel(q_ref, k_ref, v_ref, ctx_ref):
    probs = softmax_of(q_ref[...], k_ref[...]).astype(jnp.bfloat16)
    ctx_ref[...] = dot(probs, v_ref[...]).astype(jnp.bfloat16)


def backward_kernel(count, q_ref, k_ref, v_ref, *refs):
    parts, (gq_ref, gk_ref, gv_ref) = refs[:count], refs[count:]
    total = parts[0][...]
    for part in parts[1:]:
        total = total + part[...].astype(jnp.float32)
    dctx = total.astype(jnp.bfloat16)
    q, k = q_ref[...], k_ref[...]
    probs = softmax_of(q, k)
    grad_probs = dot(dctx, v_ref[...], NT)
    inner = jnp.sum(probs * grad_probs, axis=-1, keepdims=True)
    grad_scores = (probs * (grad_probs - inner) * SCALING).astype(jnp.bfloat16)
    gq_ref[...] = dot(grad_scores, k).astype(jnp.bfloat16)
    gk_ref[...] = dot(grad_scores, q, TN).astype(jnp.bfloat16)
    gv_ref[...] = dot(probs.astype(jnp.bfloat16), dctx, TN).astype(jnp.bfloat16)


def per_head(kernel, operands, outs):
    rows, width = operands[0].shape
    block = pl.BlockSpec((PATCHES, HEAD_DIM), lambda i, h: (i, h))
    shape = jax.ShapeDtypeStruct((rows, width), jnp.bfloat16)
    area = rows * PATCHES * width
    return pl.pallas_call(
        kernel,
        grid=(rows // PATCHES, width // HEAD_DIM),
        in_specs=[block] * len(operands),
        out_specs=[block] * outs,
        out_shape=[shape] * outs,
        cost_estimate=pl.CostEstimate(
            flops=4 * outs * area,
            bytes_accessed=2 * (len(operands) + outs) * rows * width,
            transcendentals=rows * PATCHES * width // HEAD_DIM,
        ),
    )(*operands)


def adam_update(grad_weight, master, moment_one, moment_two):
    new_one = 0.9 * moment_one + 0.1 * grad_weight
    new_two = 0.95 * moment_two + 0.05 * grad_weight * grad_weight
    new_master = master - 0.001 * (new_one / 0.19) / (jnp.sqrt(new_two / 0.0975) + 1e-08)
    return (new_master, new_one, new_two)


def local(queries, keys, values, cotangent, master, moment_one, moment_two):
    bf16 = jnp.bfloat16
    B = PAIR
    A = lax.axis_size("dp") // B
    M = lax.axis_size("mp")
    d = lax.axis_index("dp")
    a, b = d // B, d % B
    m = lax.axis_index("mp")
    rows, width = queries.shape
    S, D = cotangent.shape
    C = master.shape[1]
    W = B * C

    def along_a(x, t):
        route = [(i * B + j, ((i + t) % A) * B + j) for i in range(A) for j in range(B)]
        return lax.ppermute(x, "dp", route)

    def along_b(x):
        route = [(i * B + j, i * B + 1 - j) for i in range(A) for j in range(B)]
        return lax.ppermute(x, "dp", route)

    def along_m(x, t):
        return lax.ppermute(x, "mp", [(i, (i + t) % M) for i in range(M)])

    def pick(x, i):
        return lax.dynamic_index_in_dim(x, i, 0, keepdims=False)

    cot_blocks = cotangent.reshape(S, A, W).transpose(1, 0, 2)
    rows_of = jnp.zeros((A, S, W), bf16)
    rows_of = lax.dynamic_update_index_in_dim(rows_of, pick(cot_blocks, a), a, 0)
    for t in range(1, A):
        got = along_a(pick(cot_blocks, (a + t) % A), t)
        rows_of = lax.dynamic_update_index_in_dim(rows_of, got, (a - t) % A, 0)

    mine = master.astype(bf16)
    other = along_b(mine)
    weight = jnp.where(
        b == 0, jnp.concatenate([mine, other], 1), jnp.concatenate([other, mine], 1)
    )

    (context,) = per_head(forward_kernel, [queries, keys, values], 1)
    ctx_all = jnp.zeros((A, rows, width), bf16)
    ctx_all = lax.dynamic_update_index_in_dim(ctx_all, context, a, 0)
    for t in range(1, A):
        ctx_all = lax.dynamic_update_index_in_dim(ctx_all, along_a(context, t), (a - t) % A, 0)

    cot_all = jnp.zeros((A, M, S, W), bf16)
    cot_all = lax.dynamic_update_slice_in_dim(cot_all, rows_of[:, None], m, 1)
    for s in range(1, M):
        got = along_m(rows_of, s)
        cot_all = lax.dynamic_update_slice_in_dim(cot_all, got[:, None], (m - s) % M, 1)
    cot_all = cot_all.reshape(A, rows, W)

    part = jnp.einsum("atd,kd->atk", cot_all, weight, preferred_element_type=jnp.float32)
    terms = [pick(part, a)]
    part_b = part.astype(bf16)
    for t in range(1, A):
        terms.append(along_a(pick(part_b, (a + t) % A), t))

    ctx_flat = ctx_all.reshape(A, M, S, width)
    out = jnp.einsum("amsk,kd->masd", ctx_flat, weight, preferred_element_type=jnp.float32)
    total = pick(out, m)
    out_b = out.astype(bf16)
    for s in range(1, M):
        total = total + along_m(pick(out_b, (m + s) % M), s).astype(jnp.float32)
    summed = total.astype(bf16)
    attn = jnp.zeros((S, D), bf16)
    attn = lax.dynamic_update_slice_in_dim(attn, pick(summed, a), a * W, 1)
    for t in range(1, A):
        got = along_a(pick(summed, (a + t) % A), t)
        attn = lax.dynamic_update_slice_in_dim(attn, got, ((a - t) % A) * W, 1)

    grad = jnp.einsum("atk,atd->kd", ctx_all, cot_all, preferred_element_type=jnp.float32)
    keep = lax.dynamic_slice_in_dim(grad, b * C, C, 1)
    give = lax.dynamic_slice_in_dim(grad, (1 - b) * C, C, 1).astype(bf16)
    grad_weight = keep + along_b(give).astype(jnp.float32)
    news = adam_update(grad_weight, master, moment_one, moment_two)

    grads = per_head(
        functools.partial(backward_kernel, len(terms)), [queries, keys, values, *terms], 3
    )
    return (attn, *grads, *news)


def solution(mesh):
    in_specs = (
        P("dp", "mp"),
        P("dp", "mp"),
        P("dp", "mp"),
        P(("dp", "mp"), None),
        P("mp", "dp"),
        P("mp", "dp"),
        P("mp", "dp"),
    )
    out_specs = (
        P(("dp", "mp"), None),
        P("dp", "mp"),
        P("dp", "mp"),
        P("dp", "mp"),
        P("mp", "dp"),
        P("mp", "dp"),
        P("mp", "dp"),
    )
    return jax.shard_map(local, mesh=mesh, in_specs=in_specs, out_specs=out_specs, check_vma=False)
```

```python
import functools

import jax
import jax.numpy as jnp
from jax import lax
from jax.experimental import pallas as pl
from jax.experimental.pallas import tpu as pltpu
from jax.sharding import PartitionSpec as P

HEAD_DIM = 128
PATCHES = 256
PAIR = 2
SCALING = HEAD_DIM ** (-0.5)
NT = (((1,), (1,)), ((), ()))
TN = (((0,), (0,)), ((), ()))


def dot(x, y, dims=(((1,), (0,)), ((), ()))):
    return lax.dot_general(x, y, dims, preferred_element_type=jnp.float32)


def softmax_of(q, k):
    scores = dot(q, k, NT) * SCALING
    e = jnp.exp(scores - jnp.max(scores, axis=-1, keepdims=True))
    return e / jnp.sum(e, axis=-1, keepdims=True)


MESH = pl.DeviceIdType.MESH


def tiles_of(extent, size=256):
    return size if extent % size == 0 else extent


def main_kernel(
    A, M, q_ref, k_ref, v_ref, cotb, wb,
    attn_ref, gq_ref, gk_ref, gv_ref, gw_ref,
    w2, cot_all, ctx_all, gbuf, grecv, gown, obuf, orecv, oown, summed, arecv, gwbuf, gwrecv,
    w_s, w_r, cz_s, cz_r, cy_s, cy_r, x_s, x_r, g_s, g_r, o_s, o_r, z_s, z_r, h_s, h_r,
):
    bf16, f32 = jnp.bfloat16, jnp.float32
    B = PAIR
    d, m = lax.axis_index("dp"), lax.axis_index("mp")
    a, b = d // B, d % B
    rows, width = q_ref.shape
    S, C = cotb.shape[2:]
    heads = width // HEAD_DIM

    def at_a(i):
        return (i * B + b, m)

    def at_m(i):
        return (d, i)

    partner = (a * B + 1 - b, m)

    def up_a(t):
        return lax.rem(a + t, A)

    def down_a(t):
        return lax.rem(a + A - t, A)

    def up_m(s):
        return lax.rem(m + s, M)

    def down_m(s):
        return lax.rem(m + M - s, M)

    def copy(src, dst, send, recv, device):
        return pltpu.make_async_remote_copy(
            src_ref=src, dst_ref=dst, send_sem=send, recv_sem=recv,
            device_id=device, device_id_type=MESH,
        )

    barrier = pltpu.get_barrier_semaphore()
    peers = [at_a(up_a(t)) for t in range(1, A)] + [at_m(up_m(s)) for s in range(1, M)] + [partner]
    for peer in peers:
        pl.semaphore_signal(barrier, inc=1, device_id=peer, device_id_type=MESH)
    pl.semaphore_wait(barrier, len(peers))

    sent = []

    def send(*args):
        c = copy(*args)
        c.start()
        sent.append(c)

    def arrived(slot, recv, device):
        copy(slot, slot, recv, recv, device).wait_recv()

    for t in range(1, A):
        to = up_a(t)
        send(cotb.at[to], cot_all.at[:, a, m], cz_s.at[t], cz_r.at[t], at_a(to))
    send(wb, w2.at[b], w_s.at[0], w_r.at[0], partner)
    for j in range(B):
        cot_all[j, a, m] = cotb[a, j]
    w2[b] = wb[...]

    def spread(t):
        here = down_a(t)
        for s in range(1, M):
            slot = cot_all.at[:, here, m]
            send(slot, slot, cy_s.at[t, s], cy_r.at[t, s], at_m(up_m(s)))

    spread(0)

    @pl.loop(0, heads)
    def _(h):
        cols = pl.ds(pl.multiple_of(h * HEAD_DIM, HEAD_DIM), HEAD_DIM)
        for i in range(rows // PATCHES):
            r = pl.ds(i * PATCHES, PATCHES)
            probs = softmax_of(q_ref[r, cols], k_ref[r, cols]).astype(bf16)
            ctx_all[a, r, cols] = dot(probs, v_ref[r, cols]).astype(bf16)

    for t in range(1, A):
        arrived(cot_all.at[:, down_a(t), m], cz_r.at[t], at_a(down_a(t)))
        spread(t)
    for t in range(1, A):
        send(ctx_all.at[a], ctx_all.at[a], x_s.at[t], x_r.at[t], at_a(up_a(t)))

    arrived(w2.at[1 - b], w_r.at[0], partner)
    kt = tiles_of(width)
    for t in [*range(1, A), 0]:
        for_a = up_a(t)
        from_t = (A - t) % A
        for s in range(1, M):
            arrived(cot_all.at[:, for_a, down_m(s)], cy_r.at[from_t, s], at_m(down_m(s)))

        @pl.loop(0, width // kt)
        def _(i):
            ks = pl.ds(pl.multiple_of(i * kt, kt), kt)
            total = dot(cot_all[0, for_a].reshape(rows, C), w2[0, ks, :], NT)
            for j in range(1, B):
                total = total + dot(cot_all[j, for_a].reshape(rows, C), w2[j, ks, :], NT)
            if t == 0:
                gown[:, ks] = total
            else:
                gbuf[t, :, ks] = total.astype(bf16)

        if t:
            send(gbuf.at[t], grecv.at[t], g_s.at[t], g_r.at[t], at_a(for_a))

    for t in range(1, A):
        arrived(ctx_all.at[down_a(t)], x_r.at[t], at_a(down_a(t)))

    ct = tiles_of(C)

    def out_terms(s):
        r = pl.ds(pl.multiple_of(up_m(s) * S, S), S)

        for c in range(C // ct):
            cs = pl.ds(c * ct, ct)
            lhs = ctx_all[:, r, :].reshape(A * S, width)
            for j in range(B):
                term = dot(lhs, w2[j, :, cs]).reshape(A, S, ct)
                if s == 0:
                    oown[j, :, :, cs] = term
                else:
                    obuf[s, j, :, :, cs] = term.astype(bf16)

        if s:
            send(obuf.at[s], orecv.at[s], o_s.at[s], o_r.at[s], at_m(up_m(s)))

    def weight_terms(half, put):
        @pl.loop(0, width // kt)
        def _(i):
            ks = pl.ds(pl.multiple_of(i * kt, kt), kt)
            lhs = ctx_all[:, :, ks].reshape(A * rows, kt)
            rhs = cot_all[half].reshape(A * rows, C)
            put(ks, dot(lhs, rhs, TN))

    for s in range(1, M):
        out_terms(s)

    def put_give(ks, value):
        gwbuf[ks, :] = value.astype(bf16)

    def put_keep(ks, value):
        gw_ref[ks, :] = value

    weight_terms(1 - b, put_give)
    send(gwbuf, gwrecv, h_s.at[0], h_r.at[0], partner)
    out_terms(0)
    weight_terms(b, put_keep)

    for s in range(1, M):
        arrived(orecv.at[s], o_r.at[s], at_m(down_m(s)))

    @pl.loop(0, A)
    def _(i):
        for j in range(B):
            total = oown[j, i]
            for s in range(1, M):
                total = total + orecv[s, j, i].astype(f32)
            summed[j, i] = total.astype(bf16)

    for t in range(1, A):
        send(summed.at[:, up_a(t)], arecv.at[t], z_s.at[t], z_r.at[t], at_a(up_a(t)))
    for j in range(B):
        attn_ref[a, j] = summed[j, a]

    for t in range(1, A):
        arrived(grecv.at[t], g_r.at[t], at_a(down_a(t)))

    @pl.loop(0, heads)
    def _(h):
        cols = pl.ds(pl.multiple_of(h * HEAD_DIM, HEAD_DIM), HEAD_DIM)
        for i in range(rows // PATCHES):
            r = pl.ds(i * PATCHES, PATCHES)
            total = gown[r, cols]
            for t in range(1, A):
                total = total + grecv[t, r, cols].astype(f32)
            dctx = total.astype(bf16)
            q, k = q_ref[r, cols], k_ref[r, cols]
            probs = softmax_of(q, k)
            grad_probs = dot(dctx, v_ref[r, cols], NT)
            inner = jnp.sum(probs * grad_probs, axis=-1, keepdims=True)
            grad_scores = (probs * (grad_probs - inner) * SCALING).astype(bf16)
            gq_ref[r, cols] = dot(grad_scores, k).astype(bf16)
            gk_ref[r, cols] = dot(grad_scores, q, TN).astype(bf16)
            gv_ref[r, cols] = dot(probs.astype(bf16), dctx, TN).astype(bf16)

    arrived(gwrecv, h_r.at[0], partner)

    @pl.loop(0, width // kt)
    def _(i):
        ks = pl.ds(pl.multiple_of(i * kt, kt), kt)
        gw_ref[ks, :] = gw_ref[ks, :] + gwrecv[ks, :].astype(f32)

    for t in range(1, A):
        arrived(arecv.at[t], z_r.at[t], at_a(down_a(t)))
        for j in range(B):
            attn_ref[down_a(t), j] = arecv[t, j]
    for c in sent:
        c.wait_send()


def adam_update(grad_weight, master, moment_one, moment_two):
    new_one = 0.9 * moment_one + 0.1 * grad_weight
    new_two = 0.95 * moment_two + 0.05 * grad_weight * grad_weight
    new_master = master - 0.001 * (new_one / 0.19) / (jnp.sqrt(new_two / 0.0975) + 1e-08)
    return (new_master, new_one, new_two)


def local(queries, keys, values, cotangent, master, moment_one, moment_two):
    bf16, f32 = jnp.bfloat16, jnp.float32
    B = PAIR
    A = lax.axis_size("dp") // B
    M = lax.axis_size("mp")
    rows, width = queries.shape
    S, D = cotangent.shape
    C = master.shape[1]
    cot_blocks = cotangent.reshape(S, A, B, C).transpose(1, 2, 0, 3)
    vmem = pl.BlockSpec(memory_space=pltpu.VMEM)
    dma = pltpu.SemaphoreType.DMA
    act = jax.ShapeDtypeStruct((rows, width), bf16)
    attn, gq, gk, gv, grad_weight = pl.pallas_call(
        functools.partial(main_kernel, A, M),
        in_specs=[vmem] * 5,
        out_specs=[vmem] * 5,
        out_shape=[
            jax.ShapeDtypeStruct((A, B, S, C), bf16), act, act, act,
            jax.ShapeDtypeStruct((width, C), f32),
        ],
        scratch_shapes=[
            pltpu.VMEM((B, width, C), bf16),
            pltpu.VMEM((B, A, M, S, C), bf16),
            pltpu.VMEM((A, rows, width), bf16),
            pltpu.VMEM((A, rows, width), bf16),
            pltpu.VMEM((A, rows, width), bf16),
            pltpu.VMEM((rows, width), f32),
            pltpu.VMEM((M, B, A, S, C), bf16),
            pltpu.VMEM((M, B, A, S, C), bf16),
            pltpu.VMEM((B, A, S, C), f32),
            pltpu.VMEM((B, A, S, C), bf16),
            pltpu.VMEM((A, B, S, C), bf16),
            pltpu.VMEM((width, C), bf16),
            pltpu.VMEM((width, C), bf16),
            dma((1,)), dma((1,)),
            dma((A,)), dma((A,)),
            dma((A, M)), dma((A, M)),
            dma((A,)), dma((A,)),
            dma((A,)), dma((A,)),
            dma((M,)), dma((M,)),
            dma((A,)), dma((A,)),
            dma((1,)), dma((1,)),
        ],
        compiler_params=pltpu.CompilerParams(
            collective_id=0, has_side_effects=True, vmem_limit_bytes=56 * 2**20
        ),
        cost_estimate=pl.CostEstimate(
            flops=6 * A * rows * width * B * C,
            bytes_accessed=16 * rows * width + 8 * width * C,
            transcendentals=2 * rows * PATCHES * width // HEAD_DIM,
        ),
    )(queries, keys, values, cot_blocks, master.astype(bf16))
    attn_out = attn.transpose(2, 0, 1, 3).reshape(S, D)
    news = adam_update(grad_weight, master, moment_one, moment_two)
    return (attn_out, gq, gk, gv, *news)


def solution(mesh):
    in_specs = (
        P("dp", "mp"),
        P("dp", "mp"),
        P("dp", "mp"),
        P(("dp", "mp"), None),
        P("mp", "dp"),
        P("mp", "dp"),
        P("mp", "dp"),
    )
    out_specs = (
        P(("dp", "mp"), None),
        P("dp", "mp"),
        P("dp", "mp"),
        P("dp", "mp"),
        P("mp", "dp"),
        P("mp", "dp"),
        P("mp", "dp"),
    )
    return jax.shard_map(local, mesh=mesh, in_specs=in_specs, out_specs=out_specs, check_vma=False)
```

```python
import functools

import jax
import jax.numpy as jnp
from jax import lax
from jax.experimental import pallas as pl
from jax.experimental.pallas import tpu as pltpu
from jax.sharding import PartitionSpec as P

HEAD_DIM = 128
PATCHES = 256
PAIR = 2
SCALING = HEAD_DIM ** (-0.5)
NT = (((1,), (1,)), ((), ()))
TN = (((0,), (0,)), ((), ()))


def dot(x, y, dims=(((1,), (0,)), ((), ()))):
    return lax.dot_general(x, y, dims, preferred_element_type=jnp.float32)


def softmax_of(q, k):
    scores = dot(q, k, NT) * SCALING
    e = jnp.exp(scores - jnp.max(scores, axis=-1, keepdims=True))
    return e / jnp.sum(e, axis=-1, keepdims=True)


MESH = pl.DeviceIdType.MESH


def tiles_of(extent, size=256):
    return size if extent % size == 0 else extent


def main_kernel(
    A, M, q_ref, k_ref, v_ref, cotb, wb,
    attn_ref, gq_ref, gk_ref, gv_ref, gw_ref,
    w2, cot_all, ctx_all, gbuf, grecv, gown, obuf, orecv, oown, summed, arecv, gwbuf, gwrecv,
    w_s, w_r, cz_s, cz_r, cy_s, cy_r, x_s, x_r, g_s, g_r, o_s, o_r, z_s, z_r, h_s, h_r,
):
    bf16, f32 = jnp.bfloat16, jnp.float32
    B = PAIR
    d, m = lax.axis_index("dp"), lax.axis_index("mp")
    a, b = d // B, d % B
    rows, width = q_ref.shape
    C = wb.shape[1]
    direct = C % HEAD_DIM == 0
    S = cotb.shape[0] if direct else cotb.shape[2]
    heads = width // HEAD_DIM

    def at_a(i):
        return (i * B + b, m)

    def at_m(i):
        return (d, i)

    partner = (a * B + 1 - b, m)

    def up_a(t):
        return lax.rem(a + t, A)

    def down_a(t):
        return lax.rem(a + A - t, A)

    def up_m(s):
        return lax.rem(m + s, M)

    def down_m(s):
        return lax.rem(m + M - s, M)

    def copy(src, dst, send, recv, device):
        return pltpu.make_async_remote_copy(
            src_ref=src, dst_ref=dst, send_sem=send, recv_sem=recv,
            device_id=device, device_id_type=MESH,
        )

    def columns(i, j):
        return pl.ds(pl.multiple_of((i * B + j) * C, HEAD_DIM), C)

    barrier = pltpu.get_barrier_semaphore()
    peers = [at_a(up_a(t)) for t in range(1, A)] + [at_m(up_m(s)) for s in range(1, M)] + [partner]
    for peer in peers:
        pl.semaphore_signal(barrier, inc=1, device_id=peer, device_id_type=MESH)
    pl.semaphore_wait(barrier, len(peers))

    sent = []

    def send(*args):
        c = copy(*args)
        c.start()
        sent.append(c)

    def arrived(slot, recv, device):
        copy(slot, slot, recv, recv, device).wait_recv()

    for t in range(1, A):
        to = up_a(t)
        for j in range(B):
            block = cotb.at[:, columns(to, j)] if direct else cotb.at[to, j]
            send(block, cot_all.at[j, a, m], cz_s.at[t, j], cz_r.at[t, j], at_a(to))
    send(wb, w2.at[b], w_s.at[0], w_r.at[0], partner)
    for j in range(B):
        cot_all[j, a, m] = cotb[:, columns(a, j)] if direct else cotb[a, j]
    w2[b] = wb[...]

    def spread(t):
        here = down_a(t)
        for s in range(1, M):
            slot = cot_all.at[:, here, m]
            send(slot, slot, cy_s.at[t, s], cy_r.at[t, s], at_m(up_m(s)))

    spread(0)

    @pl.loop(0, heads)
    def _(h):
        cols = pl.ds(pl.multiple_of(h * HEAD_DIM, HEAD_DIM), HEAD_DIM)
        for i in range(rows // PATCHES):
            r = pl.ds(i * PATCHES, PATCHES)
            probs = softmax_of(q_ref[r, cols], k_ref[r, cols]).astype(bf16)
            ctx_all[a, r, cols] = dot(probs, v_ref[r, cols]).astype(bf16)

    for t in range(1, A):
        for j in range(B):
            arrived(cot_all.at[j, down_a(t), m], cz_r.at[t, j], at_a(down_a(t)))
        spread(t)

    def hop(way, k):
        block = ctx_all.at[a - k if way == 0 else a + k]
        to = a + 1 if way == 0 else a - 1
        origin = a - k if way == 0 else a + k
        return copy(block, block, x_s.at[way, k], x_r.at[origin], at_a(to))

    def passes(way, k):
        if way == 0:
            return (a >= k) & (a + 1 < A)
        return (a + k < A) & (a >= 1)

    def take(way, k):
        origin = a - k if way == 0 else a + k

        @pl.when(a >= k if way == 0 else a + k < A)
        def _():
            arrived(ctx_all.at[origin], x_r.at[origin], at_a(a - 1 if way == 0 else a + 1))

    def pass_on(way, k):
        @pl.when(passes(way, k))
        def _():
            hop(way, k).start()

    for k in range(A - 1):
        for way in range(2):
            if k:
                take(way, k)
            pass_on(way, k)

    arrived(w2.at[1 - b], w_r.at[0], partner)
    kt = tiles_of(width)
    for t in [*range(1, A), 0]:
        for_a = up_a(t)
        from_t = (A - t) % A
        for s in range(1, M):
            arrived(cot_all.at[:, for_a, down_m(s)], cy_r.at[from_t, s], at_m(down_m(s)))

        @pl.loop(0, width // kt)
        def _(i):
            ks = pl.ds(pl.multiple_of(i * kt, kt), kt)
            total = dot(cot_all[0, for_a].reshape(rows, C), w2[0, ks, :], NT)
            for j in range(1, B):
                total = total + dot(cot_all[j, for_a].reshape(rows, C), w2[j, ks, :], NT)
            if t == 0:
                gown[:, ks] = total
            else:
                gbuf[t, :, ks] = total.astype(bf16)

        if t:
            send(gbuf.at[t], grecv.at[t], g_s.at[t], g_r.at[t], at_a(for_a))

    for way in range(2):
        if A > 1:
            take(way, A - 1)

    ct = tiles_of(C)

    def out_terms(s):
        r = pl.ds(pl.multiple_of(up_m(s) * S, S), S)

        for c in range(C // ct):
            cs = pl.ds(c * ct, ct)
            lhs = ctx_all[:, r, :].reshape(A * S, width)
            for j in range(B):
                term = dot(lhs, w2[j, :, cs]).reshape(A, S, ct)
                if s == 0:
                    oown[j, :, :, cs] = term
                else:
                    obuf[s, j, :, :, cs] = term.astype(bf16)

        if s:
            send(obuf.at[s], orecv.at[s], o_s.at[s], o_r.at[s], at_m(up_m(s)))

    def weight_terms(half, put):
        @pl.loop(0, width // kt)
        def _(i):
            ks = pl.ds(pl.multiple_of(i * kt, kt), kt)
            lhs = ctx_all[:, :, ks].reshape(A * rows, kt)
            rhs = cot_all[half].reshape(A * rows, C)
            put(ks, dot(lhs, rhs, TN))

    for s in range(1, M):
        out_terms(s)

    def put_give(ks, value):
        gwbuf[ks, :] = value.astype(bf16)

    def put_keep(ks, value):
        gw_ref[ks, :] = value

    weight_terms(1 - b, put_give)
    send(gwbuf, gwrecv, h_s.at[0], h_r.at[0], partner)
    out_terms(0)
    weight_terms(b, put_keep)

    for s in range(1, M):
        arrived(orecv.at[s], o_r.at[s], at_m(down_m(s)))

    @pl.loop(0, A)
    def _(i):
        for j in range(B):
            total = oown[j, i]
            for s in range(1, M):
                total = total + orecv[s, j, i].astype(f32)
            summed[j, i] = total.astype(bf16)

    for t in range(1, A):
        send(summed.at[:, up_a(t)], arecv.at[t], z_s.at[t], z_r.at[t], at_a(up_a(t)))

    def put_attn(i, j, value):
        if direct:
            attn_ref[:, columns(i, j)] = value
        else:
            attn_ref[i, j] = value

    for j in range(B):
        put_attn(a, j, summed[j, a])

    for t in range(1, A):
        arrived(grecv.at[t], g_r.at[t], at_a(down_a(t)))

    @pl.loop(0, heads)
    def _(h):
        cols = pl.ds(pl.multiple_of(h * HEAD_DIM, HEAD_DIM), HEAD_DIM)
        for i in range(rows // PATCHES):
            r = pl.ds(i * PATCHES, PATCHES)
            total = gown[r, cols]
            for t in range(1, A):
                total = total + grecv[t, r, cols].astype(f32)
            dctx = total.astype(bf16)
            q, k = q_ref[r, cols], k_ref[r, cols]
            probs = softmax_of(q, k)
            grad_probs = dot(dctx, v_ref[r, cols], NT)
            inner = jnp.sum(probs * grad_probs, axis=-1, keepdims=True)
            grad_scores = (probs * (grad_probs - inner) * SCALING).astype(bf16)
            gq_ref[r, cols] = dot(grad_scores, k).astype(bf16)
            gk_ref[r, cols] = dot(grad_scores, q, TN).astype(bf16)
            gv_ref[r, cols] = dot(probs.astype(bf16), dctx, TN).astype(bf16)

    arrived(gwrecv, h_r.at[0], partner)

    @pl.loop(0, width // kt)
    def _(i):
        ks = pl.ds(pl.multiple_of(i * kt, kt), kt)
        gw_ref[ks, :] = gw_ref[ks, :] + gwrecv[ks, :].astype(f32)

    for t in range(1, A):
        arrived(arecv.at[t], z_r.at[t], at_a(down_a(t)))
        for j in range(B):
            put_attn(down_a(t), j, arecv[t, j])
    for c in sent:
        c.wait_send()
    for k in range(A - 1):
        for way in range(2):

            @pl.when(passes(way, k))
            def _():
                hop(way, k).wait_send()


def adam_update(grad_weight, master, moment_one, moment_two):
    new_one = 0.9 * moment_one + 0.1 * grad_weight
    new_two = 0.95 * moment_two + 0.05 * grad_weight * grad_weight
    new_master = master - 0.001 * (new_one / 0.19) / (jnp.sqrt(new_two / 0.0975) + 1e-08)
    return (new_master, new_one, new_two)


def local(queries, keys, values, cotangent, master, moment_one, moment_two):
    bf16, f32 = jnp.bfloat16, jnp.float32
    B = PAIR
    A = lax.axis_size("dp") // B
    M = lax.axis_size("mp")
    rows, width = queries.shape
    S, D = cotangent.shape
    C = master.shape[1]
    direct = C % HEAD_DIM == 0
    if direct:
        cot_blocks = cotangent
    else:
        cot_blocks = cotangent.reshape(S, A, B, C).transpose(1, 2, 0, 3)
    vmem = pl.BlockSpec(memory_space=pltpu.VMEM)
    dma = pltpu.SemaphoreType.DMA
    act = jax.ShapeDtypeStruct((rows, width), bf16)
    attn, gq, gk, gv, grad_weight = pl.pallas_call(
        functools.partial(main_kernel, A, M),
        in_specs=[vmem] * 5,
        out_specs=[vmem] * 5,
        out_shape=[
            jax.ShapeDtypeStruct((S, D) if direct else (A, B, S, C), bf16), act, act, act,
            jax.ShapeDtypeStruct((width, C), f32),
        ],
        scratch_shapes=[
            pltpu.VMEM((B, width, C), bf16),
            pltpu.VMEM((B, A, M, S, C), bf16),
            pltpu.VMEM((A, rows, width), bf16),
            pltpu.VMEM((A, rows, width), bf16),
            pltpu.VMEM((A, rows, width), bf16),
            pltpu.VMEM((rows, width), f32),
            pltpu.VMEM((M, B, A, S, C), bf16),
            pltpu.VMEM((M, B, A, S, C), bf16),
            pltpu.VMEM((B, A, S, C), f32),
            pltpu.VMEM((B, A, S, C), bf16),
            pltpu.VMEM((A, B, S, C), bf16),
            pltpu.VMEM((width, C), bf16),
            pltpu.VMEM((width, C), bf16),
            dma((1,)), dma((1,)),
            dma((A, B)), dma((A, B)),
            dma((A, M)), dma((A, M)),
            dma((2, A)), dma((A,)),
            dma((A,)), dma((A,)),
            dma((M,)), dma((M,)),
            dma((A,)), dma((A,)),
            dma((1,)), dma((1,)),
        ],
        compiler_params=pltpu.CompilerParams(
            collective_id=0, has_side_effects=True, vmem_limit_bytes=56 * 2**20
        ),
        cost_estimate=pl.CostEstimate(
            flops=6 * A * rows * width * B * C,
            bytes_accessed=16 * rows * width + 8 * width * C,
            transcendentals=2 * rows * PATCHES * width // HEAD_DIM,
        ),
    )(queries, keys, values, cot_blocks, master.astype(bf16))
    attn_out = attn if direct else attn.transpose(2, 0, 1, 3).reshape(S, D)
    news = adam_update(grad_weight, master, moment_one, moment_two)
    return (attn_out, gq, gk, gv, *news)


def solution(mesh):
    in_specs = (
        P("dp", "mp"),
        P("dp", "mp"),
        P("dp", "mp"),
        P(("dp", "mp"), None),
        P("mp", "dp"),
        P("mp", "dp"),
        P("mp", "dp"),
    )
    out_specs = (
        P(("dp", "mp"), None),
        P("dp", "mp"),
        P("dp", "mp"),
        P("dp", "mp"),
        P("mp", "dp"),
        P("mp", "dp"),
        P("mp", "dp"),
    )
    return jax.shard_map(local, mesh=mesh, in_specs=in_specs, out_specs=out_specs, check_vma=False)
```
